512 devices in a mesh: rows: 128 (over y_lo, z, x), cols: 4 (over y_hi, core).
Axes of the slice: x: 4, y: 4 (y_hi: 2, y_lo: 2; y = y_hi * 2 + y_lo), z: 16, core: 2. Of those that a mesh axis runs over, the one named last changes fastest.
Arguments:
- level1_basis: float32 [98304, 256], P('rows'), may hold values from -6 to 6
- level2_basis: float32 [256, 98304], P('cols', 'rows'), may hold values from -6 to 6
- probes: float32 [98304, 2048], P('rows', 'cols'), may hold values from -6 to 6
Outputs:
- solution: float32 [98304, 2048], P('rows', 'cols')
- updated_basis: float32 [256, 98304], P('cols', 'rows')
The draws below stay inside these ranges and needn't reach their ends.
All inputs are finite; a program needn't handle non-finite values.
Results may differ from the reference program's by a relative error of at most 0.0003.
Values sent between devices are 32-bit elements; how exact they have to be, the bound alone decides.
No kernel may reach another device: no remote copies, remote signals or barrier semaphores. Data moves between devices by JAX's collectives and lax.ppermute only.
A program may use at most 64 MiB of HBM per device.

```python
import math
import jax
import jax.numpy as jnp
from jax import lax

LEAF = 768
RANK = 256
POINTS = 98304
PROBES = 2048
N_ROWS = 128


def unit_entries(key, shape):
    normal_part = jnp.clip(jax.random.normal(jax.random.fold_in(key, 1), shape, jnp.float32), -6.0, 6.0)
    return normal_part


def column_scales(key, count):
    return jnp.exp(jax.random.uniform(key, (count,), jnp.float32, math.log(0.05), math.log(2.5)))


def first_basis(key):
    key = jax.random.fold_in(key, 11)
    scales = column_scales(jax.random.fold_in(key, 3), RANK)
    entries = unit_entries(jax.random.fold_in(key, 4), (POINTS, RANK))
    return jnp.clip(entries * scales[None, :], -6.0, 6.0)


def draw_level1_basis(key, part):
    return first_basis(key)


def draw_level2_basis(key, part):
    key = jax.random.fold_in(key, 23)
    scales = column_scales(jax.random.fold_in(key, 5), RANK)
    entries = unit_entries(jax.random.fold_in(key, 6), (RANK, POINTS))
    return jnp.clip(entries * scales[:, None], -6.0, 6.0)


def draw_probes(key, part):
    shared = first_basis(key)
    key = jax.random.fold_in(key, 37)
    noise = unit_entries(key, (POINTS, PROBES))
    aligned = shared[:, jnp.arange(PROBES) % RANK]
    return jnp.clip(noise + aligned, -6.0, 6.0)


def setup_inputs(seed: int = 0) -> dict:
    key_of = jax.random.split(jax.random.key(seed), 4)
    level1_basis = draw_level1_basis(jax.random.fold_in(key_of[3], 71), 0)
    level2_basis = draw_level2_basis(jax.random.fold_in(key_of[3], 71), 0)
    probes = draw_probes(jax.random.fold_in(key_of[3], 71), 0)
    return {"level1_basis": level1_basis, "level2_basis": level2_basis, "probes": probes}


PRECISE = lax.Precision.HIGHEST

def coupling_inverse(basis_rank, leaf_count):
    identity = jnp.eye(basis_rank, dtype=jnp.float32)
    upper_rows = jnp.concatenate([2.0 * identity, -identity], axis=1)
    lower_rows = jnp.concatenate([-identity, 2.0 * identity], axis=1)
    return jnp.concatenate([upper_rows, lower_rows], axis=0) * (leaf_count / 3.0)

def solve_pair(gram_low, gram_high, rhs_low, rhs_high):
    basis_rank = gram_low.shape[0]
    zero_block = jnp.zeros_like(gram_low)
    capacitance = coupling_inverse(basis_rank, LEAF) + jnp.concatenate([jnp.concatenate([gram_low, zero_block], axis=1), jnp.concatenate([zero_block, gram_high], axis=1)], axis=0)
    factor = jnp.linalg.cholesky(capacitance)
    stacked = jax.scipy.linalg.cho_solve((factor, True), jnp.concatenate([rhs_low, rhs_high], axis=0))
    return (stacked[:basis_rank], stacked[basis_rank:])

def level_one_leaf(basis_one, basis_two_t, probe_block):
    gram = jnp.einsum('lr,ls->rs', basis_one, basis_one, precision=PRECISE)
    rhs_basis = jnp.einsum('lr,kl->rk', basis_one, basis_two_t, precision=PRECISE)
    rhs_probe = jnp.einsum('lr,lk->rk', basis_one, probe_block, precision=PRECISE)
    return (gram, jnp.concatenate([rhs_basis, rhs_probe], axis=1))

def apply_one(basis_one, basis_two_t, probe_block, solved):
    updated_t = basis_two_t - jnp.einsum('rk,lr->kl', solved[:, :RANK], basis_one, precision=PRECISE)
    probe_new = probe_block - jnp.einsum('lr,rk->lk', basis_one, solved[:, RANK:], precision=PRECISE)
    return (updated_t, probe_new)

def quad_block(blocks):
    basis_one, basis_two_t, probe_block = blocks
    updated_list = []
    probe_list = []
    for pair_index in range(2):
        low = 2 * pair_index
        high = low + 1
        gram_low, rhs_low = level_one_leaf(basis_one[low], basis_two_t[low], probe_block[low])
        gram_high, rhs_high = level_one_leaf(basis_one[high], basis_two_t[high], probe_block[high])
        solved_low, solved_high = solve_pair(gram_low, gram_high, rhs_low, rhs_high)
        for leaf_index, solved in ((low, solved_low), (high, solved_high)):
            updated_t, probe_new = apply_one(basis_one[leaf_index], basis_two_t[leaf_index], probe_block[leaf_index], solved)
            updated_list.append(updated_t)
            probe_list.append(probe_new)
    grams = []
    rights = []
    for leaf_index in range(4):
        grams.append(jnp.einsum('al,bl->ab', basis_two_t[leaf_index], updated_list[leaf_index], precision=PRECISE))
        rights.append(jnp.einsum('al,lk->ak', basis_two_t[leaf_index], probe_list[leaf_index], precision=PRECISE))
    solved_low, solved_high = solve_pair(grams[0] + grams[1], grams[2] + grams[3], rights[0] + rights[1], rights[2] + rights[3])
    outputs = []
    for leaf_index in range(4):
        solved = solved_low if leaf_index < 2 else solved_high
        outputs.append(probe_list[leaf_index] - jnp.einsum('al,ak->lk', updated_list[leaf_index], solved, precision=PRECISE))
    return (jnp.stack(outputs), jnp.stack(updated_list))

def reference(level1_basis, level2_basis, probes):
    quads = N_ROWS // 4
    basis_one = level1_basis.reshape(quads, 4, LEAF, RANK)
    basis_two_t = level2_basis.reshape(RANK, quads, 4, LEAF).transpose(1, 2, 0, 3)
    probe_block = probes.reshape(quads, 4, LEAF, PROBES)
    solution, updated = lax.map(quad_block, (basis_one, basis_two_t, probe_block))
    solution = solution.reshape(POINTS, PROBES)
    updated_basis = updated.transpose(2, 0, 1, 3).reshape(RANK, POINTS)
    return (solution, updated_basis)
```

```python
import jax
import jax.numpy as jnp
from jax import lax
from jax.experimental import pallas as pl
from jax.experimental.pallas import tpu as pltpu
from jax.sharding import PartitionSpec as P

F32 = jnp.float32
BF16 = jnp.bfloat16
NN = (((1,), (0,)), ((), ()))
NT = (((1,), (1,)), ((), ()))
VMEM_BYTES = 56 * 2**20


def halves(x):
    high = x.astype(BF16)
    low = (x - high.astype(F32)).astype(BF16)
    return high, low


def pass_dot(a, b, dims):
    return lax.dot_general(a, b, dims, preferred_element_type=F32)


def dot3(a, b, dims=NN):
    a_high, a_low = halves(a)
    b_high, b_low = halves(b)
    cross = pass_dot(a_high, b_low, dims) + pass_dot(a_low, b_high, dims)
    return pass_dot(a_high, b_high, dims) + cross


def dot6(a, b, dims=NN):
    return lax.dot_general(a, b, dims, precision=lax.Precision.HIGHEST, preferred_element_type=F32)


def unit_matrix(n):
    return (lax.broadcasted_iota(jnp.int32, (n, n), 0) == lax.broadcasted_iota(jnp.int32, (n, n), 1)).astype(F32)


def invert(matrices, works, floor):
    n = matrices[0].shape[0]
    eye = unit_matrix(n)
    low = floor * 0.98
    tops = [jnp.max(jnp.sum(jnp.abs(m[...]), axis=0, keepdims=True), axis=1, keepdims=True) for m in matrices]
    top = tops[0]
    for other in tops[1:]:
        top = jnp.maximum(top, other)
    top = jnp.max(top) * 1.02
    scale = 2.0 / (top + low)
    spread = (top - low) / (top + low)
    square = spread * spread
    gain = 2.0 / (2.0 - square)
    for m, w in zip(matrices, works):
        w[...] = (gain * scale) * (2.0 * eye - scale * m[...])

    def coarse(state):
        square = state * state
        gain = 2.0 / (2.0 - square)
        for m, w in zip(matrices, works):
            x = w[...]
            w[...] = gain * (2.0 * x - dot3(x, dot3(m[...], x)))
        return square / (2.0 - square)

    lax.while_loop(lambda state: state > 1e-2, coarse, square / (2.0 - square))
    steps = jnp.where(top > 200.0 * low, 4, 2)

    def fine(_, carry):
        for m, w in zip(matrices, works):
            x = w[...]
            w[...] = x + dot3(x, eye - dot6(m[...], x))
        return carry

    lax.fori_loop(0, steps, fine, 0)


def refine_schur(schur, start):
    eye = unit_matrix(schur.shape[0])
    spread = 1.0 / 7.0
    x = start * (8.0 / 7.0)
    for step in range(2):
        square = spread * spread
        gain = 2.0 / (2.0 - square)
        spread = square / (2.0 - square)
        x = gain * (2.0 * x - dot3(x, dot3(schur, x)))
    return x + dot3(x, eye - dot6(schur, x))


def first_kernel(coupling, y1_ref, y2t_ref, z_ref, cap_ref, inv_ref, bt_ref, dd_ref, rhs_ref):
    y1 = y1_ref[...]
    y2t = y2t_ref[...]
    y1t = y1.T
    n = y1.shape[1]
    cap_ref[...] = dot6(y1t, y1) + (2.0 * coupling) * unit_matrix(n)
    bt_ref[...] = dot6(y2t, y1)
    dd_ref[...] = dot6(y2t, y2t, NT)
    z = z_ref[...]
    rhs_ref[:n] = dot3(y1t, z)
    rhs_ref[n:] = dot3(y2t, z)
    invert([cap_ref], [inv_ref], 2.0 * coupling)


def pair_kernel(coupling, cap_ref, inv_ref, bt_ref, dd_ref, other_inv_ref, other_bt_ref, t_ref, et_ref, et_other_ref, p_ref):
    other = other_inv_ref[...]
    bt = bt_ref[...]
    other_bt = other_bt_ref[...]
    t = refine_schur(cap_ref[...] - coupling * coupling * other, inv_ref[...])
    t_ref[...] = t
    et = dot6(bt + coupling * dot6(other_bt, other), t)
    et_ref[...] = et
    p_ref[...] = dd_ref[...] - dot6(et, bt, NT)
    et_other_ref[...] = dot6(other_bt + coupling * et, other)


def rhs_kernel(coupling, t_ref, et_ref, et_other_ref, other_inv_ref, rhs_ref, other_rhs_ref, f_ref, ez_ref):
    n = t_ref.shape[0]
    own = rhs_ref[:n]
    other = other_rhs_ref[:n]
    f_ref[...] = rhs_ref[n:] + other_rhs_ref[n:] - dot3(et_ref[...], own) - dot3(et_other_ref[...], other)
    ez_ref[...] = dot3(t_ref[...], own + coupling * dot3(other_inv_ref[...], other))


def quad_kernel(coupling, p_ref, t_ref, far_ref, cap_ref, far_cap_ref, own_ref):
    n = t_ref.shape[0]
    diagonal = (2.0 * coupling) * unit_matrix(n)
    cap_ref[...] = p_ref[0] + p_ref[1] + diagonal
    far_cap_ref[...] = p_ref[2] + p_ref[3] + diagonal
    invert([cap_ref, far_cap_ref], [own_ref, far_ref], 2.0 * coupling)
    t_ref[...] = refine_schur(cap_ref[...] - coupling * coupling * far_ref[...], own_ref[...])


def last_kernel(coupling, t_ref, far_ref, f_ref, f_far_ref, ez_ref, et_ref, y1_ref, y2t_ref, z_ref, out_ref):
    k = dot3(t_ref[...], f_ref[...] + coupling * dot3(far_ref[...], f_far_ref[...]))
    c1 = ez_ref[...] - dot3(et_ref[...].T, k)
    out_ref[...] = z_ref[...] - dot3(y1_ref[...], c1) - dot3(y2t_ref[...].T, k)


def updated_kernel(y2_ref, et_ref, y1_ref, out_ref):
    out_ref[...] = y2_ref[...] - dot3(et_ref[...], y1_ref[...], NT)


def call(kernel, outs, *args, **kw):
    return pl.pallas_call(
        kernel,
        out_shape=[jax.ShapeDtypeStruct(o, F32) for o in outs],
        in_specs=[pl.BlockSpec(memory_space=pltpu.VMEM)] * len(args),
        out_specs=[pl.BlockSpec(memory_space=pltpu.VMEM)] * len(outs),
        compiler_params=pltpu.CompilerParams(vmem_limit_bytes=VMEM_BYTES),
        **kw,
    )(*args)


def shards(level1_basis, level2_basis, probes):
    points, rank = level1_basis.shape
    part, columns = level2_basis.shape[0], probes.shape[1]
    coupling = points / 3.0
    n_rows = lax.axis_size("rows")
    quads = [[4 * q + i for i in range(4)] for q in range(n_rows // 4)]
    place = lax.axis_index("rows") % 4
    square = (rank, rank)

    def kern(f):
        return lambda *refs: f(coupling, *refs)

    def swap(value, bits):
        return lax.ppermute(value, "rows", [(i, i ^ bits) for i in range(n_rows)])

    y2t = lax.all_gather(level2_basis, "cols", axis=0, tiled=True)
    cap, inv, bt, dd, rhs = call(
        kern(first_kernel), [square, square, square, square, (2 * rank, columns)], level1_basis, y2t, probes
    )
    other = swap(jnp.concatenate([inv, bt], axis=0), 1)
    other_inv, other_bt = other[:rank], other[rank:]
    other_rhs = swap(rhs, 1)
    t, et, et_other, p = call(kern(pair_kernel), [square] * 4, cap, inv, bt, dd, other_inv, other_bt)
    f_own, ez = call(kern(rhs_kernel), [(rank, columns)] * 2, t, et, et_other, other_inv, rhs, other_rhs)
    all_p = lax.all_gather(p, "rows", axis_index_groups=quads)
    f_far = swap(f_own, 3)
    all_p = jnp.where(place >= 2, jnp.concatenate([all_p[2:], all_p[:2]], axis=0), all_p)
    t2, far2, _, _, _ = call(kern(quad_kernel), [square] * 5, all_p)
    (out,) = call(
        kern(last_kernel), [(points, columns)], t2, far2, f_own, f_far, ez, et, level1_basis, y2t, probes
    )
    start = lax.axis_index("cols") * part
    et_part = lax.dynamic_slice_in_dim(et, start, part, axis=0)
    (updated,) = call(updated_kernel, [(part, points)], level2_basis, et_part, level1_basis)
    return out, updated


def solution(mesh):
    return jax.shard_map(
        shards,
        mesh=mesh,
        in_specs=(P("rows", None), P("cols", "rows"), P("rows", "cols")),
        out_specs=(P("rows", "cols"), P("cols", "rows")),
        check_vma=False,
    )
```

```python
import jax
import jax.numpy as jnp
from jax import lax
from jax.experimental import pallas as pl
from jax.experimental.pallas import tpu as pltpu
from jax.sharding import PartitionSpec as P

F32 = jnp.float32
BF16 = jnp.bfloat16
NN = (((1,), (0,)), ((), ()))
NT = (((1,), (1,)), ((), ()))
VMEM_BYTES = 56 * 2**20


def halves(x):
    high = x.astype(BF16)
    low = (x - high.astype(F32)).astype(BF16)
    return high, low


def pass_dot(a, b, dims):
    return lax.dot_general(a, b, dims, preferred_element_type=F32)


def dot3(a, b, dims=NN):
    a_high, a_low = halves(a)
    b_high, b_low = halves(b)
    cross = pass_dot(a_high, b_low, dims) + pass_dot(a_low, b_high, dims)
    return pass_dot(a_high, b_high, dims) + cross


def dot6(a, b, dims=NN):
    return lax.dot_general(a, b, dims, precision=lax.Precision.HIGHEST, preferred_element_type=F32)


def unit_matrix(n):
    return (lax.broadcasted_iota(jnp.int32, (n, n), 0) == lax.broadcasted_iota(jnp.int32, (n, n), 1)).astype(F32)


def invert(matrices, works, floor):
    n = matrices[0].shape[0]
    eye = unit_matrix(n)
    low = floor * 0.98
    tops = [jnp.max(jnp.sum(jnp.abs(m[...]), axis=0, keepdims=True), axis=1, keepdims=True) for m in matrices]
    top = tops[0]
    for other in tops[1:]:
        top = jnp.maximum(top, other)
    top = jnp.max(top) * 1.02
    scale = 2.0 / (top + low)
    spread = (top - low) / (top + low)
    square = spread * spread
    gain = 2.0 / (2.0 - square)
    for m, w in zip(matrices, works):
        w[...] = (gain * scale) * (2.0 * eye - scale * m[...])

    def coarse(state):
        square = state * state
        gain = 2.0 / (2.0 - square)
        for m, w in zip(matrices, works):
            x = w[...]
            w[...] = gain * (2.0 * x - dot3(x, dot3(m[...], x)))
        return square / (2.0 - square)

    lax.while_loop(lambda state: state > 1e-2, coarse, square / (2.0 - square))
    steps = jnp.where(top > 200.0 * low, 4, 2)

    def fine(_, carry):
        for m, w in zip(matrices, works):
            x = w[...]
            w[...] = x + dot3(x, eye - dot6(m[...], x))
        return carry

    lax.fori_loop(0, steps, fine, 0)


def refine_schur(schur, start):
    eye = unit_matrix(schur.shape[0])
    spread = 1.0 / 7.0
    x = start * (8.0 / 7.0)
    for step in range(2):
        square = spread * spread
        gain = 2.0 / (2.0 - square)
        spread = square / (2.0 - square)
        x = gain * (2.0 * x - dot3(x, dot3(schur, x)))
    return x + dot3(x, eye - dot6(schur, x))


def leaf_kernel(coupling, y1_ref, z_ref, cap_ref, y_ref):
    y1 = y1_ref[...]
    y1t = y1.T
    cap_ref[...] = dot6(y1t, y1) + (2.0 * coupling) * unit_matrix(y1.shape[1])
    y_ref[...] = dot3(y1t, z_ref[...])


def invert_kernel(coupling, cap_ref, inv_ref):
    invert([cap_ref], [inv_ref], 2.0 * coupling)


def cross_kernel(coupling, y1_ref, near_ref, far_ref, inv_ref, bt_ref, sent_ref, dd_ref):
    y2t = jnp.concatenate([near_ref[...], far_ref[...]], axis=0)
    bt = dot6(y2t, y1_ref[...])
    bt_ref[...] = bt
    sent_ref[...] = jnp.where(lax.axis_index("cols") % 2 == 0, inv_ref[...], bt)
    dd_ref[...] = dot6(y2t, y2t, NT)


def project_kernel(coupling, near_ref, far_ref, z_ref, bt_ref, w_ref):
    z = z_ref[...]
    half = near_ref.shape[0]
    w_ref[:half] = dot3(near_ref[...], z)
    w_ref[half:] = dot3(far_ref[...], z)


def pair_kernel(coupling, cap_ref, inv_ref, bt_ref, other_ref, dd_ref, t_ref, et_ref, p_ref):
    n = cap_ref.shape[0]
    bt = bt_ref[...]
    other_inv = other_ref[:n]
    t = refine_schur(cap_ref[...] - coupling * coupling * other_inv, inv_ref[...])
    t_ref[...] = t
    et = dot6(bt + coupling * dot6(other_ref[n:], other_inv), t)
    et_ref[...] = et
    p_ref[...] = dd_ref[...] - dot6(et, bt, NT)


def rhs_kernel(coupling, t_ref, et_ref, other_ref, y_ref, other_y_ref, w_ref, other_w_ref, f_ref, ez_ref):
    n = t_ref.shape[0]
    own = y_ref[...]
    other = other_y_ref[...]
    et = et_ref[...]
    other_inv = other_ref[:n]
    et_other = dot3(other_ref[n:] + coupling * et, other_inv)
    f_ref[...] = w_ref[...] + other_w_ref[...] - dot3(et, own) - dot3(et_other, other)
    ez_ref[...] = dot3(t_ref[...], own + coupling * dot3(other_inv, other))


def apply_kernel(coupling, y1_ref, near_ref, far_ref, z_ref, et_ref, ez_ref, z1_ref, ut_ref, updated_ref):
    y1 = y1_ref[...]
    half = near_ref.shape[0]
    part = updated_ref.shape[0]
    change = dot3(et_ref[...], y1, NT)
    ut_ref[:half] = near_ref[...] - change[:half]
    ut_ref[half:] = far_ref[...] - change[half:]
    start = (lax.axis_index("cols") % 2) * part
    updated_ref[...] = ut_ref[pl.ds(pl.multiple_of(start, part), part), :]
    z1_ref[...] = z_ref[...] - dot3(y1, ez_ref[...])


def quad_kernel(coupling, p_ref, other_p_ref, cap_ref, inv_ref):
    cap_ref[...] = p_ref[...] + other_p_ref[...] + (2.0 * coupling) * unit_matrix(p_ref.shape[0])
    invert([cap_ref], [inv_ref], 2.0 * coupling)


def last_kernel(coupling, cap_ref, inv_ref, far_ref, f_ref, f_far_ref, z1_ref, ut_ref, out_ref):
    far = far_ref[...]
    t = refine_schur(cap_ref[...] - coupling * coupling * far, inv_ref[...])
    k = dot3(t, f_ref[...] + coupling * dot3(far, f_far_ref[...]))
    out_ref[...] = z1_ref[...] - dot3(ut_ref[...].T, k)


def call(kernel, outs, *args, micros=5):
    return pl.pallas_call(
        kernel,
        out_shape=[jax.ShapeDtypeStruct(o, F32) for o in outs],
        in_specs=[pl.BlockSpec(memory_space=pltpu.VMEM)] * len(args),
        out_specs=[pl.BlockSpec(memory_space=pltpu.VMEM)] * len(outs),
        compiler_params=pltpu.CompilerParams(vmem_limit_bytes=VMEM_BYTES),
        cost_estimate=pl.CostEstimate(flops=int(micros * 1e9), bytes_accessed=int(micros * 3e6), transcendentals=0),
    )(*args)


def shards(level1_basis, level2_basis, probes):
    points, rank = level1_basis.shape
    part, columns = level2_basis.shape[0], probes.shape[1]
    coupling = points / 3.0
    n_cols = lax.axis_size("cols")
    square, wide = (rank, rank), (rank, columns)

    def run(kernel, outs, *args, micros):
        return call(lambda *refs: kernel(coupling, *refs), outs, *args, micros=micros)

    def swap(value, bits, axis="rows"):
        return lax.ppermute(value, axis, [(i, i ^ bits) for i in range(lax.axis_size(axis))])

    def core_gather(value):
        groups = [[2 * i, 2 * i + 1] for i in range(n_cols // 2)]
        return lax.all_gather(value, "cols", axis=0, tiled=True, axis_index_groups=groups)

    near = core_gather(level2_basis)
    far = swap(near, 2, "cols")
    cap, y = run(leaf_kernel, [square, wide], level1_basis, probes, micros=4)
    other_y = swap(y, 1)
    (inv,) = run(invert_kernel, [square], cap, micros=10)
    bt, sent, dd = run(cross_kernel, [square] * 3, level1_basis, near, far, inv, micros=3)
    other_half = swap(sent, 1)
    (w,) = run(project_kernel, [wide], near, far, probes, bt, micros=3)
    other_w = swap(w, 1)
    other = core_gather(other_half)
    t, et, p = run(pair_kernel, [square] * 3, cap, inv, bt, other, dd, micros=20)
    other_p = swap(p, 1)
    f, ez = run(rhs_kernel, [wide] * 2, t, et, other, y, other_y, w, other_w, micros=4)
    f_far = swap(f, 3)
    cap_two, inv_two = run(quad_kernel, [square] * 2, p, other_p, micros=6)
    far_two = swap(inv_two, 3)
    z1, ut, updated = run(
        apply_kernel, [(points, columns), (rank, points), (part, points)], level1_basis, near, far, probes, et, ez, micros=4
    )
    (out,) = run(last_kernel, [(points, columns)], cap_two, inv_two, far_two, f, f_far, z1, ut, micros=7)
    return out, updated


def solution(mesh):
    return jax.shard_map(
        shards,
        mesh=mesh,
        in_specs=(P("rows", None), P("cols", "rows"), P("rows", "cols")),
        out_specs=(P("rows", "cols"), P("cols", "rows")),
        check_vma=False,
    )
```

```python
import jax
import jax.numpy as jnp
from jax import lax
from jax.experimental import pallas as pl
from jax.experimental.pallas import tpu as pltpu
from jax.sharding import PartitionSpec as P

F32 = jnp.float32
BF16 = jnp.bfloat16
NN = (((1,), (0,)), ((), ()))
NT = (((1,), (1,)), ((), ()))
VMEM_BYTES = 20 * 2**20


def halves(x):
    high = x.astype(BF16)
    low = (x - high.astype(F32)).astype(BF16)
    return high, low


def pass_dot(a, b, dims):
    return lax.dot_general(a, b, dims, preferred_element_type=F32)


def dot3(a, b, dims=NN):
    a_high, a_low = halves(a)
    b_high, b_low = halves(b)
    cross = pass_dot(a_high, b_low, dims) + pass_dot(a_low, b_high, dims)
    return pass_dot(a_high, b_high, dims) + cross


def dot6(a, b, dims=NN):
    return lax.dot_general(a, b, dims, precision=lax.Precision.HIGHEST, preferred_element_type=F32)


def unit_matrix(n):
    return (lax.broadcasted_iota(jnp.int32, (n, n), 0) == lax.broadcasted_iota(jnp.int32, (n, n), 1)).astype(F32)


def invert(matrices, works, floor):
    n = matrices[0].shape[0]
    eye = unit_matrix(n)
    low = floor * 0.98
    tops = [jnp.max(jnp.sum(jnp.abs(m[...]), axis=0, keepdims=True), axis=1, keepdims=True) for m in matrices]
    top = tops[0]
    for other in tops[1:]:
        top = jnp.maximum(top, other)
    top = jnp.max(top) * 1.02
    scale = 2.0 / (top + low)
    spread = (top - low) / (top + low)
    square = spread * spread
    gain = 2.0 / (2.0 - square)
    for m, w in zip(matrices, works):
        w[...] = (gain * scale) * (2.0 * eye - scale * m[...])

    def coarse(state):
        square = state * state
        gain = 2.0 / (2.0 - square)
        for m, w in zip(matrices, works):
            x = w[...]
            w[...] = gain * (2.0 * x - dot3(x, dot3(m[...], x)))
        return square / (2.0 - square)

    lax.while_loop(lambda state: state > 1e-2, coarse, square / (2.0 - square))
    wide = top > 256.0 * low
    steps = jnp.where(wide, 4, 2)

    def fine(_, carry):
        for m, w in zip(matrices, works):
            x = w[...]
            w[...] = x + dot3(x, eye - dot6(m[...], x))
        return carry

    lax.fori_loop(0, steps, fine, 0)
    return wide


def flag(wide):
    return jnp.broadcast_to(jnp.where(wide, 1.0, 0.0), (8, 128)).astype(F32)


def refine_schur(schur, start):
    eye = unit_matrix(schur.shape[0])
    spread = 1.0 / 7.0
    x = start * (8.0 / 7.0)
    for step in range(2):
        square = spread * spread
        gain = 2.0 / (2.0 - square)
        spread = square / (2.0 - square)
        x = gain * (2.0 * x - dot3(x, dot3(schur, x)))
    return x + dot3(x, eye - dot6(schur, x))


def leaf_kernel(coupling, y1_ref, z_ref, cap_ref, y_ref):
    y1 = y1_ref[...]
    y1t = y1.T
    cap_ref[...] = dot6(y1t, y1) + (2.0 * coupling) * unit_matrix(y1.shape[1])
    y_ref[...] = dot3(y1t, z_ref[...])


def invert_kernel(coupling, cap_ref, inv_ref, wide_ref):
    wide_ref[...] = flag(invert([cap_ref], [inv_ref], 2.0 * coupling))


def cross_kernel(coupling, wide_ref, y1_ref, near_ref, far_ref, cap_ref, inv_ref, bt_ref, ht_ref, sent_ref, dd_ref):
    y2t = jnp.concatenate([near_ref[...], far_ref[...]], axis=0)
    bt_ref[...] = dot6(y2t, y1_ref[...])
    ht_ref[...] = dot6(bt_ref[...], inv_ref[...])

    @pl.when(wide_ref[0, 0] > 0.5)
    def _():
        h = ht_ref[...]
        ht_ref[...] = h + dot3(bt_ref[...] - dot6(h, cap_ref[...]), inv_ref[...])

    sent_ref[...] = jnp.where(lax.axis_index("cols") % 2 == 0, inv_ref[...], ht_ref[...])
    dd_ref[...] = dot6(y2t, y2t, NT)


def project_kernel(coupling, near_ref, far_ref, z_ref, y_ref, ht_ref, w_ref, v_ref):
    z = z_ref[...]
    half = near_ref.shape[0]
    w_ref[:half] = dot3(near_ref[...], z)
    w_ref[half:] = dot3(far_ref[...], z)
    v_ref[...] = w_ref[...] - dot3(ht_ref[...], y_ref[...])


def pair_kernel(coupling, wide_ref, cap_ref, inv_ref, bt_ref, other_ref, dd_ref, schur_ref, t_ref, et_ref, p_ref):
    n = cap_ref.shape[0]
    bt = bt_ref[...]
    schur_ref[...] = cap_ref[...] - coupling * coupling * other_ref[:n]
    t_ref[...] = refine_schur(schur_ref[...], inv_ref[...])
    et_ref[...] = dot6(bt + coupling * other_ref[n:], t_ref[...])

    @pl.when(wide_ref[0, 0] > 0.5)
    def _():
        et = et_ref[...]
        et_ref[...] = et + dot3(bt_ref[...] + coupling * other_ref[n:] - dot6(et, schur_ref[...]), t_ref[...])

    p_ref[...] = dd_ref[...] - dot6(et_ref[...], bt, NT)


def rhs_kernel(coupling, wide_ref, schur_ref, t_ref, et_ref, y_ref, other_ref, other_y_ref, w_ref, other_v_ref, f_ref, ez_ref):
    n = t_ref.shape[0]
    g = y_ref[...] + coupling * dot3(other_ref[:n], other_y_ref[...])
    f_ref[...] = w_ref[...] + other_v_ref[...] - dot3(et_ref[...], g)
    ez_ref[...] = dot3(t_ref[...], g)

    @pl.when(wide_ref[0, 0] > 0.5)
    def _():
        e = ez_ref[...]
        ez_ref[...] = e + dot3(t_ref[...], g - dot6(schur_ref[...], e))


def apply_kernel(coupling, y1_ref, near_ref, far_ref, z_ref, et_ref, ez_ref, z1_ref, high_ref, low_ref, updated_ref, ut_ref):
    y1 = y1_ref[...]
    half = near_ref.shape[0]
    part = updated_ref.shape[0]
    change = dot3(et_ref[...], y1, NT)
    ut_ref[:half] = near_ref[...] - change[:half]
    ut_ref[half:] = far_ref[...] - change[half:]
    start = (lax.axis_index("cols") % 2) * part
    updated_ref[...] = ut_ref[pl.ds(pl.multiple_of(start, part), part), :]
    high_ref[...], low_ref[...] = halves(ut_ref[...].T)
    z1_ref[...] = z_ref[...] - dot3(y1, ez_ref[...])


def quad_kernel(coupling, p_ref, other_p_ref, cap_ref, inv_ref, wide_ref):
    cap_ref[...] = p_ref[...] + other_p_ref[...] + (2.0 * coupling) * unit_matrix(p_ref.shape[0])
    wide_ref[...] = flag(invert([cap_ref], [inv_ref], 2.0 * coupling))


def last_kernel(coupling, wide_ref, cap_ref, inv_ref, far_ref, f_ref, f_far_ref, z1_ref, high_ref, low_ref, out_ref, k_ref):
    schur = cap_ref[...] - coupling * coupling * far_ref[...]
    t = refine_schur(schur, inv_ref[...])
    g = f_ref[...] + coupling * dot3(far_ref[...], f_far_ref[...])
    k_ref[...] = dot3(t, g)

    @pl.when(wide_ref[0, 0] > 0.5)
    def _():
        k = k_ref[...]
        k_ref[...] = k + dot3(t, g - dot6(schur, k))

    k_high, k_low = halves(k_ref[...])
    high = high_ref[...]
    change = pass_dot(high, k_low, NN) + pass_dot(low_ref[...], k_high, NN)
    out_ref[...] = z1_ref[...] - pass_dot(high, k_high, NN) - change


def call(kernel, outs, *args, micros, scratch=()):
    return pl.pallas_call(
        kernel,
        out_shape=[o if isinstance(o, jax.ShapeDtypeStruct) else jax.ShapeDtypeStruct(o, F32) for o in outs],
        in_specs=[pl.BlockSpec(memory_space=pltpu.VMEM)] * len(args),
        out_specs=[pl.BlockSpec(memory_space=pltpu.VMEM)] * len(outs),
        scratch_shapes=[pltpu.VMEM(shape, F32) for shape in scratch],
        compiler_params=pltpu.CompilerParams(vmem_limit_bytes=VMEM_BYTES),
        cost_estimate=pl.CostEstimate(flops=int(micros * 1e9), bytes_accessed=int(micros * 3e6), transcendentals=0),
    )(*args)


def shards(level1_basis, level2_basis, probes):
    points, rank = level1_basis.shape
    part, columns = level2_basis.shape[0], probes.shape[1]
    coupling = points / 3.0
    n_cols = lax.axis_size("cols")
    square, tall, tile = (rank, rank), (rank, columns), (8, 128)

    def run(kernel, outs, *args, **kw):
        return call(lambda *refs: kernel(coupling, *refs), outs, *args, **kw)

    def swap(value, bits, axis="rows"):
        return lax.ppermute(value, axis, [(i, i ^ bits) for i in range(lax.axis_size(axis))])

    def core_gather(value):
        groups = [[2 * i, 2 * i + 1] for i in range(n_cols // 2)]
        return lax.all_gather(value, "cols", axis=0, tiled=True, axis_index_groups=groups)

    near = core_gather(level2_basis)
    far = swap(near, 2, "cols")
    cap, y = run(leaf_kernel, [square, tall], level1_basis, probes, micros=4)
    other_y = swap(y, 1)
    inv, wide = run(invert_kernel, [square, tile], cap, micros=10)
    bt, ht, sent, dd = run(cross_kernel, [square] * 4, wide, level1_basis, near, far, cap, inv, micros=4)
    other_half = swap(sent, 1)
    w, v = run(project_kernel, [tall] * 2, near, far, probes, y, ht, micros=3)
    other_v = swap(v, 1)
    other = core_gather(other_half)
    schur, t, et, p = run(pair_kernel, [square] * 4, wide, cap, inv, bt, other, dd, micros=20)
    other_p = swap(p, 1)
    f, ez = run(rhs_kernel, [tall] * 2, wide, schur, t, et, y, other, other_y, w, other_v, micros=4)
    f_far = swap(f, 3)
    cap_two, inv_two, wide_two = run(quad_kernel, [square, square, tile], p, other_p, micros=6)
    far_two = swap(inv_two, 3)
    half = jax.ShapeDtypeStruct((points, rank), BF16)
    z1, high, low, updated = run(
        apply_kernel,
        [(points, columns), half, half, (part, points)],
        *(level1_basis, near, far, probes, et, ez),
        micros=4,
        scratch=[(rank, points)],
    )
    (out,) = run(
        last_kernel,
        [(points, columns)],
        *(wide_two, cap_two, inv_two, far_two, f, f_far, z1, high, low),
        micros=7,
        scratch=[(rank, columns)],
    )
    return out, updated


def solution(mesh):
    return jax.shard_map(
        shards,
        mesh=mesh,
        in_specs=(P("rows", None), P("cols", "rows"), P("rows", "cols")),
        out_specs=(P("rows", "cols"), P("cols", "rows")),
        check_vma=False,
    )
```

```python
import jax
import jax.numpy as jnp
from jax import lax
from jax.experimental import pallas as pl
from jax.experimental.pallas import tpu as pltpu
from jax.sharding import PartitionSpec as P

F32 = jnp.float32
BF16 = jnp.bfloat16
NN = (((1,), (0,)), ((), ()))
NT = (((1,), (1,)), ((), ()))
VMEM_BYTES = 20 * 2**20


def halves(x):
    high = x.astype(BF16)
    low = (x - high.astype(F32)).astype(BF16)
    return high, low


def pass_dot(a, b, dims):
    return lax.dot_general(a, b, dims, preferred_element_type=F32)


def dot3(a, b, dims=NN):
    a_high, a_low = halves(a)
    b_high, b_low = halves(b)
    cross = pass_dot(a_high, b_low, dims) + pass_dot(a_low, b_high, dims)
    return pass_dot(a_high, b_high, dims) + cross


def dot6(a, b, dims=NN):
    return lax.dot_general(a, b, dims, precision=lax.Precision.HIGHEST, preferred_element_type=F32)


def unit_matrix(n):
    return (lax.broadcasted_iota(jnp.int32, (n, n), 0) == lax.broadcasted_iota(jnp.int32, (n, n), 1)).astype(F32)


def invert(matrix, floor, store, pair):
    n = matrix.shape[0]
    eye = unit_matrix(n)
    low = floor * 0.98
    top = jnp.max(jnp.sum(jnp.abs(matrix[...]), axis=0, keepdims=True)) * 1.02
    scale = 2.0 / (top + low)
    spread = (top - low) / (top + low)
    narrow = top < 64.0 * low
    wide = top > 256.0 * low

    @pl.when(narrow)
    def _():
        pair[:n] = scale * eye
        pair[n:] = eye - scale * matrix[...]

        def step(state):
            square = state * state
            gain = 2.0 / (2.0 - square)
            both = pair[...]
            product = dot3(both, both[n:])
            pair[:n] = gain * (both[:n] + product[:n])
            pair[n:] = (1.0 - gain) * eye + gain * product[n:]
            return square / (2.0 - square)

        lax.while_loop(lambda state: state > 1e-3, step, spread)
        x = pair[:n]
        store[...] = x + dot3(x, eye - dot6(matrix[...], x))

    @pl.when(jnp.logical_not(narrow))
    def _():
        store[...] = scale * eye

        def coarse(state):
            square = state * state
            gain = 2.0 / (2.0 - square)
            x = store[...]
            store[...] = gain * (2.0 * x - dot3(x, dot3(matrix[...], x)))
            return square / (2.0 - square)

        lax.while_loop(lambda state: state > 1e-2, coarse, spread)

        def fine(_, carry):
            x = store[...]
            store[...] = x + dot3(x, eye - dot6(matrix[...], x))
            return carry

        lax.fori_loop(0, jnp.where(wide, 4, 2), fine, 0)

    return wide


def flag(wide):
    return jnp.broadcast_to(jnp.where(wide, 1.0, 0.0), (8, 128)).astype(F32)


def refine_schur(schur, start):
    x = start * (8.0 / 7.0)
    r = unit_matrix(schur.shape[0]) - dot6(schur, x)
    r_two = dot3(r, r)
    x = x + dot6(x, r)
    r_four = dot3(r_two, r_two)
    x = x + dot3(x, r_two)
    return x + dot3(x, r_four)


def pack(matrix, out_ref):
    n = matrix.shape[0] // 2
    out_ref[:n] = matrix[:n, :n]
    out_ref[n : 2 * n] = 0.5 * (matrix[n:, :n] + matrix[:n, n:].T)
    out_ref[2 * n :] = matrix[n:, n:]


def unpack(packed):
    n = packed.shape[1]
    low = packed[n : 2 * n]
    top = jnp.concatenate([packed[:n], low.T], axis=1)
    return jnp.concatenate([top, jnp.concatenate([low, packed[2 * n :]], axis=1)], axis=0)


def leaf_kernel(coupling, y1_hbm, z_hbm, part_hbm, cap_ref, y_ref, part_ref, y1_ref, z_ref, sems):
    load_y1 = pltpu.make_async_copy(y1_hbm, y1_ref, sems.at[0])
    load_z = pltpu.make_async_copy(z_hbm, z_ref, sems.at[1])
    load_part = pltpu.make_async_copy(part_hbm, part_ref, sems.at[2])
    load_y1.start()
    load_z.start()
    load_part.start()
    load_y1.wait()
    y1 = y1_ref[...]
    y1t = y1.T
    cap_ref[...] = dot6(y1t, y1) + (2.0 * coupling) * unit_matrix(y1.shape[1])
    load_z.wait()
    y_ref[...] = dot3(y1t, z_ref[...])
    load_part.wait()


def invert_kernel(coupling, cap_ref, inv_ref, wide_ref, pair_ref):
    wide_ref[...] = flag(invert(cap_ref, 2.0 * coupling, inv_ref, pair_ref))


def cross_kernel(coupling, wide_ref, y1_ref, y2t_ref, cap_ref, inv_ref, bt_ref, ht_ref, sent_ref, dd_ref):
    y2t = y2t_ref[...]
    bt_ref[...] = dot6(y2t, y1_ref[...])
    ht_ref[...] = dot6(bt_ref[...], inv_ref[...])

    @pl.when(wide_ref[0, 0] > 0.5)
    def _():
        h = ht_ref[...]
        ht_ref[...] = h + dot3(bt_ref[...] - dot6(h, cap_ref[...]), inv_ref[...])

    sent_ref[...] = jnp.where(lax.axis_index("cols") % 2 == 0, inv_ref[...], ht_ref[...])
    dd_ref[...] = dot6(y2t, y2t, NT)


def project_kernel(coupling, y2t_ref, z_ref, y_ref, ht_ref, w_ref, v_ref):
    w_ref[...] = dot3(y2t_ref[...], z_ref[...])
    v_ref[...] = w_ref[...] - dot3(ht_ref[...], y_ref[...])


def pair_kernel(coupling, wide_ref, cap_ref, inv_ref, bt_ref, other_ref, dd_ref, schur_ref, t_ref, et_ref, p_ref):
    n = cap_ref.shape[0]
    bt = bt_ref[...]
    schur_ref[...] = cap_ref[...] - coupling * coupling * other_ref[:n]
    t_ref[...] = refine_schur(schur_ref[...], inv_ref[...])
    et_ref[...] = dot6(bt + coupling * other_ref[n:], t_ref[...])

    @pl.when(wide_ref[0, 0] > 0.5)
    def _():
        et = et_ref[...]
        et_ref[...] = et + dot3(bt_ref[...] + coupling * other_ref[n:] - dot6(et, schur_ref[...]), t_ref[...])

    pack(dd_ref[...] - dot6(et_ref[...], bt, NT), p_ref)


def rhs_kernel(coupling, wide_ref, schur_ref, t_ref, et_ref, y_ref, other_ref, other_y_ref, w_ref, other_v_ref, f_ref, ez_ref):
    n = t_ref.shape[0]
    g = y_ref[...] + coupling * dot3(other_ref[:n], other_y_ref[...])
    f_ref[...] = w_ref[...] + other_v_ref[...] - dot3(et_ref[...], g)
    ez_ref[...] = dot3(t_ref[...], g)

    @pl.when(wide_ref[0, 0] > 0.5)
    def _():
        e = ez_ref[...]
        ez_ref[...] = e + dot3(t_ref[...], g - dot6(schur_ref[...], e))


def apply_kernel(coupling, y1_ref, y2t_ref, z_ref, et_ref, ez_ref, z1_ref, high_ref, low_ref, updated_ref, ut_ref):
    y1 = y1_ref[...]
    part = updated_ref.shape[0]
    ut_ref[...] = y2t_ref[...] - dot3(et_ref[...], y1, NT)
    start = (lax.axis_index("cols") % 2) * (2 * part)
    updated_ref[...] = ut_ref[pl.ds(pl.multiple_of(start, part), part), :]
    high_ref[...], low_ref[...] = halves(ut_ref[...].T)
    z1_ref[...] = z_ref[...] - dot3(y1, ez_ref[...])


def quad_kernel(coupling, p_ref, other_p_ref, cap_ref, inv_ref, wide_ref, sent_ref, pair_ref):
    cap_ref[...] = unpack(p_ref[...] + other_p_ref[...]) + (2.0 * coupling) * unit_matrix(cap_ref.shape[0])
    wide_ref[...] = flag(invert(cap_ref, 2.0 * coupling, inv_ref, pair_ref))
    pack(inv_ref[...], sent_ref)


def last_kernel(coupling, wide_ref, cap_ref, inv_ref, far_ref, f_ref, f_far_ref, z1_ref, high_ref, low_ref, out_hbm, k_ref, out_ref, sems):
    far = unpack(far_ref[...])
    schur = cap_ref[...] - coupling * coupling * far
    t = refine_schur(schur, inv_ref[...])
    g = f_ref[...] + coupling * dot3(far, f_far_ref[...])
    k_ref[...] = dot3(t, g)

    @pl.when(wide_ref[0, 0] > 0.5)
    def _():
        k = k_ref[...]
        k_ref[...] = k + dot3(t, g - dot6(schur, k))

    k_high, k_low = halves(k_ref[...])
    pieces = sems.shape[0]
    rows = out_ref.shape[0] // pieces
    stores = []
    for i in range(pieces):
        block = slice(i * rows, (i + 1) * rows)
        high = high_ref[block]
        change = pass_dot(high, k_low, NN) + pass_dot(low_ref[block], k_high, NN)
        out_ref[block] = z1_ref[block] - pass_dot(high, k_high, NN) - change
        store = pltpu.make_async_copy(out_ref.at[block], out_hbm.at[block], sems.at[i])
        store.start()
        stores.append(store)
    for store in stores:
        store.wait()


def call(kernel, outs, *args, micros, scratch=(), space=pltpu.VMEM, out_space=pltpu.VMEM, grant=VMEM_BYTES):
    return pl.pallas_call(
        kernel,
        out_shape=[o if isinstance(o, jax.ShapeDtypeStruct) else jax.ShapeDtypeStruct(o, F32) for o in outs],
        in_specs=[pl.BlockSpec(memory_space=space)] * len(args),
        out_specs=[pl.BlockSpec(memory_space=out_space)] * len(outs),
        scratch_shapes=[pltpu.VMEM(x, F32) if isinstance(x, tuple) else x for x in scratch],
        compiler_params=pltpu.CompilerParams(vmem_limit_bytes=grant),
        cost_estimate=pl.CostEstimate(flops=int(micros * 1e9), bytes_accessed=int(micros * 3e6), transcendentals=0),
    )(*args)


def shards(level1_basis, level2_basis, probes):
    points, rank = level1_basis.shape
    part, columns = level2_basis.shape[0], probes.shape[1]
    coupling = points / 3.0
    n_cols = lax.axis_size("cols")
    square, tall, tile = (rank, rank), (rank, columns), (8, 128)
    packed = (3 * rank // 2, rank // 2)

    def run(kernel, outs, *args, **kw):
        return call(lambda *refs: kernel(coupling, *refs), outs, *args, **kw)

    def swap(value, bits, axis="rows"):
        return lax.ppermute(value, axis, [(i, i ^ bits) for i in range(lax.axis_size(axis))])

    def core_gather(value):
        groups = [[2 * i, 2 * i + 1] for i in range(n_cols // 2)]
        return lax.all_gather(value, "cols", axis=0, tiled=True, axis_index_groups=groups)

    cap, y, own_part = run(
        leaf_kernel,
        [square, tall, (part, points)],
        *(level1_basis, probes, level2_basis),
        micros=3,
        scratch=[(points, rank), (points, columns), pltpu.SemaphoreType.DMA((3,))],
        space=pltpu.HBM,
        grant=62 * 2**20,
    )
    far_part = swap(own_part, 2, "cols")
    other_y = swap(y, 1)
    inv, wide = run(invert_kernel, [square, tile], cap, micros=4, scratch=[(2 * rank, rank)])
    y2t = core_gather(jnp.concatenate([own_part, far_part], axis=0))
    bt, ht, sent, dd = run(cross_kernel, [square] * 4, wide, level1_basis, y2t, cap, inv, micros=4)
    other_half = swap(sent, 1)
    w, v = run(project_kernel, [tall] * 2, y2t, probes, y, ht, micros=3)
    other_v = swap(v, 1)
    other = core_gather(other_half)
    schur, t, et, p = run(pair_kernel, [square] * 3 + [packed], wide, cap, inv, bt, other, dd, micros=20)
    other_p = swap(p, 1)
    f, ez = run(rhs_kernel, [tall] * 2, wide, schur, t, et, y, other, other_y, w, other_v, micros=4)
    f_far = swap(f, 3)
    cap_two, inv_two, wide_two, sent_two = run(
        quad_kernel, [square, square, tile, packed], p, other_p, micros=6, scratch=[(2 * rank, rank)]
    )
    far_two = swap(sent_two, 3)
    half = jax.ShapeDtypeStruct((points, rank), BF16)
    z1, high, low, updated = run(
        apply_kernel,
        [(points, columns), half, half, (part, points)],
        *(level1_basis, y2t, probes, et, ez),
        micros=4,
        scratch=[(rank, points)],
    )
    (out,) = run(
        last_kernel,
        [(points, columns)],
        *(wide_two, cap_two, inv_two, far_two, f, f_far, z1, high, low),
        micros=7,
        scratch=[(rank, columns), (points, columns), pltpu.SemaphoreType.DMA((3,))],
        out_space=pltpu.HBM,
    )
    return out, updated


def solution(mesh):
    return jax.shard_map(
        shards,
        mesh=mesh,
        in_specs=(P("rows", None), P("cols", "rows"), P("rows", "cols")),
        out_specs=(P("rows", "cols"), P("cols", "rows")),
        check_vma=False,
    )
```

```python
import functools

import jax
import jax.numpy as jnp
from jax import lax
from jax.experimental import pallas as pl
from jax.experimental.pallas import tpu as pltpu
from jax.sharding import PartitionSpec as P

F32 = jnp.float32
BF16 = jnp.bfloat16
NN = (((1,), (0,)), ((), ()))
NT = (((1,), (1,)), ((), ()))
VMEM_BYTES = 20 * 2**20


def halves(x):
    high = x.astype(BF16)
    low = (x - high.astype(F32)).astype(BF16)
    return high, low


def pass_dot(a, b, dims):
    return lax.dot_general(a, b, dims, preferred_element_type=F32)


def dot3(a, b, dims=NN):
    a_high, a_low = halves(a)
    b_high, b_low = halves(b)
    cross = pass_dot(a_high, b_low, dims) + pass_dot(a_low, b_high, dims)
    return pass_dot(a_high, b_high, dims) + cross


def dot6(a, b, dims=NN):
    return lax.dot_general(a, b, dims, precision=lax.Precision.HIGHEST, preferred_element_type=F32)


def unit_matrix(n):
    return (lax.broadcasted_iota(jnp.int32, (n, n), 0) == lax.broadcasted_iota(jnp.int32, (n, n), 1)).astype(F32)


def invert(matrix, floor, store, pair):
    n = matrix.shape[0]
    eye = unit_matrix(n)
    low = floor * 0.98
    top = jnp.max(jnp.sum(jnp.abs(matrix[...]), axis=0, keepdims=True)) * 1.02
    scale = 2.0 / (top + low)
    spread = (top - low) / (top + low)
    narrow = top < 64.0 * low
    wide = top > 256.0 * low

    @pl.when(narrow)
    def _():
        pair[:n] = scale * eye
        pair[n:] = eye - scale * matrix[...]

        def step(state):
            square = state * state
            gain = 2.0 / (2.0 - square)
            both = pair[...]
            product = dot3(both, both[n:])
            pair[:n] = gain * (both[:n] + product[:n])
            pair[n:] = (1.0 - gain) * eye + gain * product[n:]
            return square / (2.0 - square)

        lax.while_loop(lambda state: state > 1e-3, step, spread)
        x = pair[:n]
        store[...] = x + dot3(x, eye - dot6(matrix[...], x))

    @pl.when(jnp.logical_not(narrow))
    def _():
        store[...] = scale * eye

        def coarse(state):
            square = state * state
            gain = 2.0 / (2.0 - square)
            x = store[...]
            store[...] = gain * (2.0 * x - dot3(x, dot3(matrix[...], x)))
            return square / (2.0 - square)

        lax.while_loop(lambda state: state > 1e-2, coarse, spread)

        def fine(_, carry):
            x = store[...]
            store[...] = x + dot3(x, eye - dot6(matrix[...], x))
            return carry

        lax.fori_loop(0, jnp.where(wide, 4, 2), fine, 0)

    return wide


def flag(wide):
    return jnp.broadcast_to(jnp.where(wide, 1.0, 0.0), (8, 128)).astype(F32)


def refine_schur(schur, start):
    x = start * (8.0 / 7.0)
    r = unit_matrix(schur.shape[0]) - dot6(schur, x)
    r_two = dot3(r, r)
    x = x + dot3(x, r)
    r_four = dot3(r_two, r_two)
    x = x + dot3(x, r_two)
    return x + dot3(x, r_four)


def pack(matrix, out_ref):
    n = matrix.shape[0] // 2
    out_ref[:n] = matrix[:n, :n]
    out_ref[n : 2 * n] = 0.5 * (matrix[n:, :n] + matrix[:n, n:].T)
    out_ref[2 * n :] = matrix[n:, n:]


def unpack(packed):
    n = packed.shape[1]
    low = packed[n : 2 * n]
    top = jnp.concatenate([packed[:n], low.T], axis=1)
    return jnp.concatenate([top, jnp.concatenate([low, packed[2 * n :]], axis=1)], axis=0)


def leaf_kernel(coupling, y1_hbm, z_hbm, part_hbm, cap_ref, y_ref, part_ref, y1_ref, z_ref, sems):
    load_y1 = pltpu.make_async_copy(y1_hbm, y1_ref, sems.at[0])
    load_z = pltpu.make_async_copy(z_hbm, z_ref, sems.at[1])
    load_part = pltpu.make_async_copy(part_hbm, part_ref, sems.at[2])
    load_y1.start()
    load_z.start()
    load_part.start()
    load_y1.wait()
    y1 = y1_ref[...]
    y1t = y1.T
    cap_ref[...] = dot6(y1t, y1) + (2.0 * coupling) * unit_matrix(y1.shape[1])
    load_z.wait()
    y_ref[...] = dot3(y1t, z_ref[...])
    load_part.wait()


def invert_kernel(coupling, cap_ref, inv_ref, wide_ref, pair_ref):
    wide_ref[...] = flag(invert(cap_ref, 2.0 * coupling, inv_ref, pair_ref))


def cross_kernel(coupling, wide_ref, y1_ref, y2t_ref, cap_ref, inv_ref, bt_ref, ht_ref, sent_ref, dd_ref):
    y2t = y2t_ref[...]
    bt_ref[...] = dot6(y2t, y1_ref[...])
    ht_ref[...] = dot6(bt_ref[...], inv_ref[...])

    @pl.when(wide_ref[0, 0] > 0.5)
    def _():
        h = ht_ref[...]
        ht_ref[...] = h + dot3(bt_ref[...] - dot6(h, cap_ref[...]), inv_ref[...])

    sent_ref[...] = jnp.where(lax.axis_index("cols") % 2 == 0, inv_ref[...], ht_ref[...])
    dd_ref[...] = dot6(y2t, y2t, NT)


def project_kernel(coupling, y2t_ref, z_ref, y_ref, ht_ref, w_ref, left_ref, right_ref):
    w_ref[...] = dot3(y2t_ref[...], z_ref[...])
    v = w_ref[...] - dot3(ht_ref[...], y_ref[...])
    half = left_ref.shape[1]
    left_ref[...] = v[:, :half]
    right_ref[...] = v[:, half:]


def pair_kernel(coupling, wide_ref, cap_ref, inv_ref, bt_ref, other_ref, dd_ref, schur_ref, t_ref, et_ref, p_ref):
    n = cap_ref.shape[0]
    bt = bt_ref[...]
    schur_ref[...] = cap_ref[...] - coupling * coupling * other_ref[:n]
    t_ref[...] = refine_schur(schur_ref[...], inv_ref[...])
    et_ref[...] = dot6(bt + coupling * other_ref[n:], t_ref[...])

    @pl.when(wide_ref[0, 0] > 0.5)
    def _():
        et = et_ref[...]
        et_ref[...] = et + dot3(bt_ref[...] + coupling * other_ref[n:] - dot6(et, schur_ref[...]), t_ref[...])

    pack(dd_ref[...] - dot6(et_ref[...], bt, NT), p_ref)


def rhs_kernel(coupling, first, wide_ref, schur_ref, t_ref, et_ref, y_ref, other_ref, other_y_ref, w_ref, other_v_ref, f_ref, ez_ref):
    n = t_ref.shape[0]
    columns = slice(first, first + f_ref.shape[1])
    g = y_ref[:, columns] + coupling * dot3(other_ref[:n], other_y_ref[:, columns])
    f_ref[...] = w_ref[:, columns] + other_v_ref[...] - dot3(et_ref[...], g)
    ez_ref[...] = dot3(t_ref[...], g)

    @pl.when(wide_ref[0, 0] > 0.5)
    def _():
        e = ez_ref[...]
        ez_ref[...] = e + dot3(t_ref[...], g - dot6(schur_ref[...], e))


def apply_kernel(coupling, y1_ref, y2t_ref, z_ref, et_ref, left_ref, right_ref, z1_ref, high_ref, low_ref, updated_ref, ut_ref):
    y1 = y1_ref[...]
    part = updated_ref.shape[0]
    ut_ref[...] = y2t_ref[...] - dot3(et_ref[...], y1, NT)
    start = (lax.axis_index("cols") % 2) * (2 * part)
    updated_ref[...] = ut_ref[pl.ds(pl.multiple_of(start, part), part), :]
    high_ref[...], low_ref[...] = halves(ut_ref[...].T)
    half = left_ref.shape[1]
    z1_ref[:, :half] = z_ref[:, :half] - dot3(y1, left_ref[...])
    z1_ref[:, half:] = z_ref[:, half:] - dot3(y1, right_ref[...])


def quad_kernel(coupling, p_ref, other_p_ref, cap_ref, inv_ref, wide_ref, sent_ref, pair_ref):
    cap_ref[...] = unpack(p_ref[...] + other_p_ref[...]) + (2.0 * coupling) * unit_matrix(cap_ref.shape[0])
    wide_ref[...] = flag(invert(cap_ref, 2.0 * coupling, inv_ref, pair_ref))
    pack(inv_ref[...], sent_ref)


def last_kernel(coupling, wide_ref, cap_ref, inv_ref, far_ref, *refs):
    left_ref, right_ref, left_far_ref, right_far_ref, z1_ref, high_ref, low_ref, out_hbm, k_ref, out_ref, sems = refs
    far = unpack(far_ref[...])
    schur = cap_ref[...] - coupling * coupling * far
    t = refine_schur(schur, inv_ref[...])
    g_left = left_ref[...] + coupling * dot3(far, left_far_ref[...])
    g_right = right_ref[...] + coupling * dot3(far, right_far_ref[...])
    half = left_ref.shape[1]
    k_ref[:, :half] = dot3(t, g_left)
    k_ref[:, half:] = dot3(t, g_right)

    @pl.when(wide_ref[0, 0] > 0.5)
    def _():
        for g, columns in ((g_left, slice(None, half)), (g_right, slice(half, None))):
            k = k_ref[:, columns]
            k_ref[:, columns] = k + dot3(t, g - dot6(schur, k))

    k_high, k_low = halves(k_ref[...])
    pieces = sems.shape[0]
    rows = out_ref.shape[0] // pieces
    stores = []
    for i in range(pieces):
        block = slice(i * rows, (i + 1) * rows)
        high = high_ref[block]
        change = pass_dot(high, k_low, NN) + pass_dot(low_ref[block], k_high, NN)
        out_ref[block] = z1_ref[block] - pass_dot(high, k_high, NN) - change
        store = pltpu.make_async_copy(out_ref.at[block], out_hbm.at[block], sems.at[i])
        store.start()
        stores.append(store)
    for store in stores:
        store.wait()


def call(kernel, outs, *args, micros, scratch=(), space=pltpu.VMEM, out_space=pltpu.VMEM, grant=VMEM_BYTES):
    return pl.pallas_call(
        kernel,
        out_shape=[o if isinstance(o, jax.ShapeDtypeStruct) else jax.ShapeDtypeStruct(o, F32) for o in outs],
        in_specs=[pl.BlockSpec(memory_space=space)] * len(args),
        out_specs=[pl.BlockSpec(memory_space=out_space)] * len(outs),
        scratch_shapes=[pltpu.VMEM(x, F32) if isinstance(x, tuple) else x for x in scratch],
        compiler_params=pltpu.CompilerParams(vmem_limit_bytes=grant),
        cost_estimate=pl.CostEstimate(flops=int(micros * 1e9), bytes_accessed=int(micros * 3e6), transcendentals=0),
    )(*args)


def shards(level1_basis, level2_basis, probes):
    points, rank = level1_basis.shape
    part, columns = level2_basis.shape[0], probes.shape[1]
    coupling = points / 3.0
    n_cols = lax.axis_size("cols")
    square, tall, tile = (rank, rank), (rank, columns), (8, 128)
    packed = (3 * rank // 2, rank // 2)

    def run(kernel, outs, *args, **kw):
        return call(lambda *refs: kernel(coupling, *refs), outs, *args, **kw)

    def swap(value, bits, axis="rows"):
        return lax.ppermute(value, axis, [(i, i ^ bits) for i in range(lax.axis_size(axis))])

    def core_gather(value):
        groups = [[2 * i, 2 * i + 1] for i in range(n_cols // 2)]
        return lax.all_gather(value, "cols", axis=0, tiled=True, axis_index_groups=groups)

    cap, y, own_part = run(
        leaf_kernel,
        [square, tall, (part, points)],
        *(level1_basis, probes, level2_basis),
        micros=3,
        scratch=[(points, rank), (points, columns), pltpu.SemaphoreType.DMA((3,))],
        space=pltpu.HBM,
        grant=62 * 2**20,
    )
    far_part = swap(own_part, 2, "cols")
    other_y = swap(y, 1)
    inv, wide = run(invert_kernel, [square, tile], cap, micros=4, scratch=[(2 * rank, rank)])
    y2t = core_gather(jnp.concatenate([own_part, far_part], axis=0))
    bt, ht, sent, dd = run(cross_kernel, [square] * 4, wide, level1_basis, y2t, cap, inv, micros=4)
    other_half = swap(sent, 1)
    w, v_left, v_right = run(project_kernel, [tall, (rank, columns // 2), (rank, columns // 2)], y2t, probes, y, ht, micros=3)
    other_v_left = swap(v_left, 1)
    other_v_right = swap(v_right, 1)
    other = core_gather(other_half)
    schur, t, et, p = run(pair_kernel, [square] * 3 + [packed], wide, cap, inv, bt, other, dd, micros=20)
    other_p = swap(p, 1)
    half = columns // 2

    def rhs(first, other_v):
        kernel = functools.partial(rhs_kernel, coupling, first)
        return call(kernel, [(rank, half)] * 2, wide, schur, t, et, y, other, other_y, w, other_v, micros=3)

    f_left, ez_left = rhs(0, other_v_left)
    far_left = swap(f_left, 3)
    f_right, ez_right = rhs(half, other_v_right)
    far_right = swap(f_right, 3)
    cap_two, inv_two, wide_two, sent_two = run(
        quad_kernel, [square, square, tile, packed], p, other_p, micros=6, scratch=[(2 * rank, rank)]
    )
    far_two = swap(sent_two, 3)
    bits = jax.ShapeDtypeStruct((points, rank), BF16)
    z1, high, low, updated = run(
        apply_kernel,
        [(points, columns), bits, bits, (part, points)],
        *(level1_basis, y2t, probes, et, ez_left, ez_right),
        micros=4,
        scratch=[(rank, points)],
    )
    (out,) = run(
        last_kernel,
        [(points, columns)],
        *(wide_two, cap_two, inv_two, far_two, f_left, f_right, far_left, far_right, z1, high, low),
        micros=7,
        scratch=[(rank, columns), (points, columns), pltpu.SemaphoreType.DMA((3,))],
        out_space=pltpu.HBM,
    )
    return out, updated


def solution(mesh):
    return jax.shard_map(
        shards,
        mesh=mesh,
        in_specs=(P("rows", None), P("cols", "rows"), P("rows", "cols")),
        out_specs=(P("rows", "cols"), P("cols", "rows")),
        check_vma=False,
    )
```

```python
import functools

import jax
import jax.numpy as jnp
from jax import lax
from jax.experimental import pallas as pl
from jax.experimental.pallas import tpu as pltpu
from jax.sharding import PartitionSpec as P

F32 = jnp.float32
BF16 = jnp.bfloat16
NN = (((1,), (0,)), ((), ()))
NT = (((1,), (1,)), ((), ()))
VMEM_BYTES = 20 * 2**20


def halves(x):
    high = x.astype(BF16)
    low = (x - high.astype(F32)).astype(BF16)
    return high, low


def pass_dot(a, b, dims):
    return lax.dot_general(a, b, dims, preferred_element_type=F32)


def dot3(a, b, dims=NN):
    a_high, a_low = halves(a)
    b_high, b_low = halves(b)
    cross = pass_dot(a_high, b_low, dims) + pass_dot(a_low, b_high, dims)
    return pass_dot(a_high, b_high, dims) + cross


def dot6(a, b, dims=NN):
    return lax.dot_general(a, b, dims, precision=lax.Precision.HIGHEST, preferred_element_type=F32)


def unit_matrix(n):
    return (lax.broadcasted_iota(jnp.int32, (n, n), 0) == lax.broadcasted_iota(jnp.int32, (n, n), 1)).astype(F32)


def invert(matrix, floor, store, pair):
    n = matrix.shape[0]
    eye = unit_matrix(n)
    low = floor * 0.98
    top = jnp.max(jnp.sum(jnp.abs(matrix[...]), axis=0, keepdims=True)) * 1.02
    scale = 2.0 / (top + low)
    spread = (top - low) / (top + low)
    narrow = top < 64.0 * low
    wide = top > 256.0 * low

    @pl.when(narrow)
    def _():
        pair[:n] = scale * eye
        pair[n:] = eye - scale * matrix[...]

        def step(state):
            square = state * state
            gain = 2.0 / (2.0 - square)
            both = pair[...]
            product = dot3(both, both[n:])
            pair[:n] = gain * (both[:n] + product[:n])
            pair[n:] = (1.0 - gain) * eye + gain * product[n:]
            return square / (2.0 - square)

        lax.while_loop(lambda state: state > 1e-3, step, spread)
        x = pair[:n]
        store[...] = x + dot3(x, eye - dot6(matrix[...], x))

    @pl.when(jnp.logical_not(narrow))
    def _():
        store[...] = scale * eye

        def coarse(state):
            square = state * state
            gain = 2.0 / (2.0 - square)
            x = store[...]
            store[...] = gain * (2.0 * x - dot3(x, dot3(matrix[...], x)))
            return square / (2.0 - square)

        lax.while_loop(lambda state: state > 1e-2, coarse, spread)

        def fine(_, carry):
            x = store[...]
            store[...] = x + dot3(x, eye - dot6(matrix[...], x))
            return carry

        lax.fori_loop(0, jnp.where(wide, 4, 2), fine, 0)

    return wide


def flag(wide):
    return jnp.broadcast_to(jnp.where(wide, 1.0, 0.0), (8, 128)).astype(F32)


def refine_schur(schur, start):
    x = start * (8.0 / 7.0)
    r = unit_matrix(schur.shape[0]) - dot6(schur, x)
    r_two = dot3(r, r)
    x = x + dot3(x, r)
    r_four = dot3(r_two, r_two)
    x = x + dot3(x, r_two)
    return x + dot3(x, r_four)


def pack(matrix, out_ref):
    n = matrix.shape[0] // 2
    out_ref[:n] = matrix[:n, :n]
    out_ref[n : 2 * n] = 0.5 * (matrix[n:, :n] + matrix[:n, n:].T)
    out_ref[2 * n :] = matrix[n:, n:]


def unpack(packed):
    n = packed.shape[1]
    low = packed[n : 2 * n]
    top = jnp.concatenate([packed[:n], low.T], axis=1)
    return jnp.concatenate([top, jnp.concatenate([low, packed[2 * n :]], axis=1)], axis=0)


def leaf_kernel(coupling, y1_hbm, z_hbm, part_hbm, cap_ref, y_ref, part_ref, y1_ref, z_ref, sems):
    load_y1 = pltpu.make_async_copy(y1_hbm, y1_ref, sems.at[0])
    load_z = pltpu.make_async_copy(z_hbm, z_ref, sems.at[1])
    load_part = pltpu.make_async_copy(part_hbm, part_ref, sems.at[2])
    load_y1.start()
    load_z.start()
    load_part.start()
    load_y1.wait()
    y1 = y1_ref[...]
    y1t = y1.T
    cap_ref[...] = dot6(y1t, y1) + (2.0 * coupling) * unit_matrix(y1.shape[1])
    load_z.wait()
    y_ref[...] = dot3(y1t, z_ref[...])
    load_part.wait()


def invert_kernel(coupling, cap_ref, inv_ref, wide_ref, pair_ref):
    wide_ref[...] = flag(invert(cap_ref, 2.0 * coupling, inv_ref, pair_ref))


def cross_kernel(coupling, wide_ref, y1_ref, y2t_ref, cap_ref, inv_ref, bt_ref, ht_ref, sent_ref):
    bt_ref[...] = dot6(y2t_ref[...], y1_ref[...])
    ht_ref[...] = dot6(bt_ref[...], inv_ref[...])

    @pl.when(wide_ref[0, 0] > 0.5)
    def _():
        h = ht_ref[...]
        ht_ref[...] = h + dot3(bt_ref[...] - dot6(h, cap_ref[...]), inv_ref[...])

    sent_ref[...] = jnp.where(lax.axis_index("cols") % 2 == 0, inv_ref[...], ht_ref[...])


def project_kernel(coupling, y2t_ref, z_ref, y_ref, ht_ref, dd_ref, w_ref, left_ref, right_ref):
    y2t = y2t_ref[...]
    w_ref[...] = dot3(y2t, z_ref[...])
    v = w_ref[...] - dot3(ht_ref[...], y_ref[...])
    half = left_ref.shape[1]
    left_ref[...] = v[:, :half]
    right_ref[...] = v[:, half:]
    dd_ref[...] = dot6(y2t, y2t, NT)


def pair_kernel(coupling, wide_ref, cap_ref, inv_ref, bt_ref, other_ref, dd_ref, schur_ref, t_ref, et_ref, p_ref):
    n = cap_ref.shape[0]
    bt = bt_ref[...]
    schur_ref[...] = cap_ref[...] - coupling * coupling * other_ref[:n]
    t_ref[...] = refine_schur(schur_ref[...], inv_ref[...])
    et_ref[...] = dot6(bt + coupling * other_ref[n:], t_ref[...])

    @pl.when(wide_ref[0, 0] > 0.5)
    def _():
        et = et_ref[...]
        et_ref[...] = et + dot3(bt_ref[...] + coupling * other_ref[n:] - dot6(et, schur_ref[...]), t_ref[...])

    pack(dd_ref[...] - dot6(et_ref[...], bt, NT), p_ref)


def rhs_kernel(coupling, first, wide_ref, schur_ref, t_ref, et_ref, y_ref, other_ref, other_y_ref, w_ref, other_v_ref, f_ref, ez_ref):
    n = t_ref.shape[0]
    columns = slice(first, first + f_ref.shape[1])
    g = y_ref[:, columns] + coupling * dot3(other_ref[:n], other_y_ref[:, columns])
    f_ref[...] = w_ref[:, columns] + other_v_ref[...] - dot3(et_ref[...], g)
    ez_ref[...] = dot3(t_ref[...], g)

    @pl.when(wide_ref[0, 0] > 0.5)
    def _():
        e = ez_ref[...]
        ez_ref[...] = e + dot3(t_ref[...], g - dot6(schur_ref[...], e))


def apply_kernel(coupling, y1_ref, y2t_ref, z_ref, et_ref, left_ref, right_ref, z1_ref, high_ref, low_ref, updated_ref, ut_ref):
    y1 = y1_ref[...]
    part = updated_ref.shape[0]
    ut_ref[...] = y2t_ref[...] - dot3(et_ref[...], y1, NT)
    start = (lax.axis_index("cols") % 2) * (2 * part)
    updated_ref[...] = ut_ref[pl.ds(pl.multiple_of(start, part), part), :]
    high_ref[...], low_ref[...] = halves(ut_ref[...].T)
    half = left_ref.shape[1]
    z1_ref[:, :half] = z_ref[:, :half] - dot3(y1, left_ref[...])
    z1_ref[:, half:] = z_ref[:, half:] - dot3(y1, right_ref[...])


def quad_kernel(coupling, p_ref, other_p_ref, cap_ref, inv_ref, wide_ref, sent_ref, pair_ref):
    cap_ref[...] = unpack(p_ref[...] + other_p_ref[...]) + (2.0 * coupling) * unit_matrix(cap_ref.shape[0])
    wide_ref[...] = flag(invert(cap_ref, 2.0 * coupling, inv_ref, pair_ref))
    pack(inv_ref[...], sent_ref)


def last_kernel(coupling, wide_ref, cap_ref, inv_ref, far_ref, *refs):
    left_ref, right_ref, left_far_ref, right_far_ref, z1_ref, high_ref, low_ref, out_hbm, k_ref, out_ref, sems = refs
    far = unpack(far_ref[...])
    schur = cap_ref[...] - coupling * coupling * far
    t = refine_schur(schur, inv_ref[...])
    g_left = left_ref[...] + coupling * dot3(far, left_far_ref[...])
    g_right = right_ref[...] + coupling * dot3(far, right_far_ref[...])
    half = left_ref.shape[1]
    k_ref[:, :half] = dot3(t, g_left)
    k_ref[:, half:] = dot3(t, g_right)

    @pl.when(wide_ref[0, 0] > 0.5)
    def _():
        for g, columns in ((g_left, slice(None, half)), (g_right, slice(half, None))):
            k = k_ref[:, columns]
            k_ref[:, columns] = k + dot3(t, g - dot6(schur, k))

    k_high, k_low = halves(k_ref[...])
    pieces = sems.shape[0]
    rows = out_ref.shape[0] // pieces
    stores = []
    for i in range(pieces):
        block = slice(i * rows, (i + 1) * rows)
        high = high_ref[block]
        change = pass_dot(high, k_low, NN) + pass_dot(low_ref[block], k_high, NN)
        out_ref[block] = z1_ref[block] - pass_dot(high, k_high, NN) - change
        store = pltpu.make_async_copy(out_ref.at[block], out_hbm.at[block], sems.at[i])
        store.start()
        stores.append(store)
    for store in stores:
        store.wait()


def call(kernel, outs, *args, micros, scratch=(), space=pltpu.VMEM, out_space=pltpu.VMEM, grant=VMEM_BYTES):
    return pl.pallas_call(
        kernel,
        out_shape=[o if isinstance(o, jax.ShapeDtypeStruct) else jax.ShapeDtypeStruct(o, F32) for o in outs],
        in_specs=[pl.BlockSpec(memory_space=space)] * len(args),
        out_specs=[pl.BlockSpec(memory_space=out_space)] * len(outs),
        scratch_shapes=[pltpu.VMEM(x, F32) if isinstance(x, tuple) else x for x in scratch],
        compiler_params=pltpu.CompilerParams(vmem_limit_bytes=grant),
        cost_estimate=pl.CostEstimate(flops=int(micros * 1e9), bytes_accessed=int(micros * 3e6), transcendentals=0),
    )(*args)


def shards(level1_basis, level2_basis, probes):
    points, rank = level1_basis.shape
    part, columns = level2_basis.shape[0], probes.shape[1]
    coupling = points / 3.0
    n_cols = lax.axis_size("cols")
    square, tall, tile = (rank, rank), (rank, columns), (8, 128)
    packed = (3 * rank // 2, rank // 2)

    def run(kernel, outs, *args, **kw):
        return call(lambda *refs: kernel(coupling, *refs), outs, *args, **kw)

    def swap(value, bits, axis="rows"):
        return lax.ppermute(value, axis, [(i, i ^ bits) for i in range(lax.axis_size(axis))])

    def core_gather(value):
        groups = [[2 * i, 2 * i + 1] for i in range(n_cols // 2)]
        return lax.all_gather(value, "cols", axis=0, tiled=True, axis_index_groups=groups)

    cap, y, own_part = run(
        leaf_kernel,
        [square, tall, (part, points)],
        *(level1_basis, probes, level2_basis),
        micros=3,
        scratch=[(points, rank), (points, columns), pltpu.SemaphoreType.DMA((3,))],
        space=pltpu.HBM,
        grant=62 * 2**20,
    )
    far_part = swap(own_part, 2, "cols")
    other_y = swap(y, 1)
    inv, wide = run(invert_kernel, [square, tile], cap, micros=4, scratch=[(2 * rank, rank)])
    y2t = core_gather(jnp.concatenate([own_part, far_part], axis=0))
    bt, ht, sent = run(cross_kernel, [square] * 3, wide, level1_basis, y2t, cap, inv, micros=4)
    other_half = swap(sent, 1)
    side = (rank, columns // 2)
    dd, w, v_left, v_right = run(project_kernel, [square, tall, side, side], y2t, probes, y, ht, micros=3)
    other_v_left = swap(v_left, 1)
    other_v_right = swap(v_right, 1)
    other = core_gather(other_half)
    schur, t, et, p = run(pair_kernel, [square] * 3 + [packed], wide, cap, inv, bt, other, dd, micros=20)
    other_p = swap(p, 1)
    half = columns // 2

    def rhs(first, other_v):
        kernel = functools.partial(rhs_kernel, coupling, first)
        return call(kernel, [(rank, half)] * 2, wide, schur, t, et, y, other, other_y, w, other_v, micros=3)

    f_left, ez_left = rhs(0, other_v_left)
    far_left = swap(f_left, 3)
    f_right, ez_right = rhs(half, other_v_right)
    far_right = swap(f_right, 3)
    cap_two, inv_two, wide_two, sent_two = run(
        quad_kernel, [square, square, tile, packed], p, other_p, micros=6, scratch=[(2 * rank, rank)]
    )
    far_two = swap(sent_two, 3)
    bits = jax.ShapeDtypeStruct((points, rank), BF16)
    z1, high, low, updated = run(
        apply_kernel,
        [(points, columns), bits, bits, (part, points)],
        *(level1_basis, y2t, probes, et, ez_left, ez_right),
        micros=4,
        scratch=[(rank, points)],
    )
    (out,) = run(
        last_kernel,
        [(points, columns)],
        *(wide_two, cap_two, inv_two, far_two, f_left, f_right, far_left, far_right, z1, high, low),
        micros=7,
        scratch=[(rank, columns), (points, columns), pltpu.SemaphoreType.DMA((3,))],
        out_space=pltpu.HBM,
    )
    return out, updated


def solution(mesh):
    return jax.shard_map(
        shards,
        mesh=mesh,
        in_specs=(P("rows", None), P("cols", "rows"), P("rows", "cols")),
        out_specs=(P("rows", "cols"), P("cols", "rows")),
        check_vma=False,
    )
```

```python
import functools

import jax
import jax.numpy as jnp
from jax import lax
from jax.experimental import pallas as pl
from jax.experimental.pallas import tpu as pltpu
from jax.sharding import PartitionSpec as P

F32 = jnp.float32
BF16 = jnp.bfloat16
NN = (((1,), (0,)), ((), ()))
NT = (((1,), (1,)), ((), ()))
VMEM_BYTES = 20 * 2**20


def halves(x):
    high = x.astype(BF16)
    low = (x - high.astype(F32)).astype(BF16)
    return high, low


def pass_dot(a, b, dims):
    return lax.dot_general(a, b, dims, preferred_element_type=F32)


def dot3(a, b, dims=NN):
    a_high, a_low = halves(a)
    b_high, b_low = halves(b)
    cross = pass_dot(a_high, b_low, dims) + pass_dot(a_low, b_high, dims)
    return pass_dot(a_high, b_high, dims) + cross


def dot6(a, b, dims=NN):
    return lax.dot_general(a, b, dims, precision=lax.Precision.HIGHEST, preferred_element_type=F32)


def unit_matrix(n):
    return (lax.broadcasted_iota(jnp.int32, (n, n), 0) == lax.broadcasted_iota(jnp.int32, (n, n), 1)).astype(F32)


def invert(matrix, floor, store, pair):
    n = matrix.shape[0]
    eye = unit_matrix(n)
    low = floor * 0.98
    top = jnp.max(jnp.sum(jnp.abs(matrix[...]), axis=0, keepdims=True)) * 1.02
    scale = 2.0 / (top + low)
    spread = (top - low) / (top + low)
    narrow = top < 64.0 * low
    wide = top > 256.0 * low

    @pl.when(narrow)
    def _():
        pair[:n] = scale * eye
        pair[n:] = eye - scale * matrix[...]

        def step(state):
            square = state * state
            gain = 2.0 / (2.0 - square)
            both = pair[...]
            product = dot3(both, both[n:])
            pair[:n] = gain * (both[:n] + product[:n])
            pair[n:] = (1.0 - gain) * eye + gain * product[n:]
            return square / (2.0 - square)

        lax.while_loop(lambda state: state > 2e-4, step, spread)
        x = pair[:n]
        store[...] = x + dot3(x, eye - dot6(matrix[...], x))

    @pl.when(jnp.logical_not(narrow))
    def _():
        store[...] = scale * eye

        def coarse(state):
            square = state * state
            gain = 2.0 / (2.0 - square)
            x = store[...]
            store[...] = gain * (2.0 * x - dot3(x, dot3(matrix[...], x)))
            return square / (2.0 - square)

        lax.while_loop(lambda state: state > 1e-2, coarse, spread)

        def fine(_, carry):
            x = store[...]
            store[...] = x + dot3(x, eye - dot6(matrix[...], x))
            return carry

        lax.fori_loop(0, jnp.where(wide, 4, 2), fine, 0)

    return wide


def flag(wide):
    return jnp.broadcast_to(jnp.where(wide, 1.0, 0.0), (8, 128)).astype(F32)


def refine_schur(schur, start):
    x = start * (8.0 / 7.0)
    r = unit_matrix(schur.shape[0]) - dot6(schur, x)
    r_two = dot3(r, r)
    x = x + dot3(x, r)
    r_four = dot3(r_two, r_two)
    x = x + dot3(x, r_two)
    return x + dot3(x, r_four)


def pack(matrix, out_ref):
    n = matrix.shape[0] // 2
    out_ref[:n] = matrix[:n, :n]
    out_ref[n : 2 * n] = 0.5 * (matrix[n:, :n] + matrix[:n, n:].T)
    out_ref[2 * n :] = matrix[n:, n:]


def unpack(packed):
    n = packed.shape[1]
    low = packed[n : 2 * n]
    top = jnp.concatenate([packed[:n], low.T], axis=1)
    return jnp.concatenate([top, jnp.concatenate([low, packed[2 * n :]], axis=1)], axis=0)


def leaf_kernel(coupling, y1_hbm, z_hbm, part_hbm, cap_ref, y_ref, part_ref, y1_ref, z_ref, sems):
    load_y1 = pltpu.make_async_copy(y1_hbm, y1_ref, sems.at[0])
    load_z = pltpu.make_async_copy(z_hbm, z_ref, sems.at[1])
    load_part = pltpu.make_async_copy(part_hbm, part_ref, sems.at[2])
    load_y1.start()
    load_z.start()
    load_part.start()
    load_y1.wait()
    y1 = y1_ref[...]
    y1t = y1.T
    cap_ref[...] = dot6(y1t, y1) + (2.0 * coupling) * unit_matrix(y1.shape[1])
    load_z.wait()
    y_ref[...] = dot3(y1t, z_ref[...])
    load_part.wait()


def invert_kernel(coupling, cap_ref, inv_ref, wide_ref, pair_ref):
    wide_ref[...] = flag(invert(cap_ref, 2.0 * coupling, inv_ref, pair_ref))


def cross_kernel(coupling, wide_ref, y1_ref, y2t_ref, cap_ref, inv_ref, bt_ref, ht_ref, sent_ref):
    bt_ref[...] = dot6(y2t_ref[...], y1_ref[...])
    ht_ref[...] = dot6(bt_ref[...], inv_ref[...])

    @pl.when(wide_ref[0, 0] > 0.5)
    def _():
        h = ht_ref[...]
        ht_ref[...] = h + dot3(bt_ref[...] - dot6(h, cap_ref[...]), inv_ref[...])

    sent_ref[...] = jnp.where(lax.axis_index("cols") % 2 == 0, inv_ref[...], ht_ref[...])


def project_kernel(coupling, y2t_ref, z_ref, y_ref, ht_ref, dd_ref, w_ref, left_ref, right_ref):
    y2t = y2t_ref[...]
    w_ref[...] = dot3(y2t, z_ref[...])
    v = w_ref[...] - dot3(ht_ref[...], y_ref[...])
    half = left_ref.shape[1]
    left_ref[...] = v[:, :half]
    right_ref[...] = v[:, half:]
    dd_ref[...] = dot6(y2t, y2t, NT)


def pair_kernel(coupling, wide_ref, cap_ref, inv_ref, bt_ref, other_ref, dd_ref, schur_ref, t_ref, et_ref, p_ref):
    n = cap_ref.shape[0]
    bt = bt_ref[...]
    schur_ref[...] = cap_ref[...] - coupling * coupling * other_ref[:n]
    t_ref[...] = refine_schur(schur_ref[...], inv_ref[...])
    et_ref[...] = dot6(bt + coupling * other_ref[n:], t_ref[...])

    @pl.when(wide_ref[0, 0] > 0.5)
    def _():
        et = et_ref[...]
        et_ref[...] = et + dot3(bt_ref[...] + coupling * other_ref[n:] - dot6(et, schur_ref[...]), t_ref[...])

    pack(dd_ref[...] - dot6(et_ref[...], bt, NT), p_ref)


def rhs_kernel(coupling, first, wide_ref, schur_ref, t_ref, et_ref, y_ref, other_ref, other_y_ref, w_ref, other_v_ref, f_ref, ez_ref):
    n = t_ref.shape[0]
    columns = slice(first, first + f_ref.shape[1])
    g = y_ref[:, columns] + coupling * dot3(other_ref[:n], other_y_ref[:, columns])
    f_ref[...] = w_ref[:, columns] + other_v_ref[...] - dot3(et_ref[...], g)
    ez_ref[...] = dot3(t_ref[...], g)

    @pl.when(wide_ref[0, 0] > 0.5)
    def _():
        e = ez_ref[...]
        ez_ref[...] = e + dot3(t_ref[...], g - dot6(schur_ref[...], e))


def apply_kernel(coupling, y1_ref, y2t_ref, z_ref, et_ref, left_ref, right_ref, z1_ref, high_ref, low_ref, updated_ref, ut_ref):
    y1 = y1_ref[...]
    part = updated_ref.shape[0]
    ut_ref[...] = y2t_ref[...] - dot3(et_ref[...], y1, NT)
    start = (lax.axis_index("cols") % 2) * (2 * part)
    updated_ref[...] = ut_ref[pl.ds(pl.multiple_of(start, part), part), :]
    high_ref[...], low_ref[...] = halves(ut_ref[...].T)
    half = left_ref.shape[1]
    z1_ref[:, :half] = z_ref[:, :half] - dot3(y1, left_ref[...])
    z1_ref[:, half:] = z_ref[:, half:] - dot3(y1, right_ref[...])


def quad_kernel(coupling, p_ref, other_p_ref, cap_ref, inv_ref, wide_ref, sent_ref, pair_ref):
    cap_ref[...] = unpack(p_ref[...] + other_p_ref[...]) + (2.0 * coupling) * unit_matrix(cap_ref.shape[0])
    wide_ref[...] = flag(invert(cap_ref, 2.0 * coupling, inv_ref, pair_ref))
    pack(inv_ref[...], sent_ref)


def last_kernel(coupling, wide_ref, cap_ref, inv_ref, far_ref, *refs):
    left_ref, right_ref, left_far_ref, right_far_ref, z1_ref, high_ref, low_ref, out_hbm, k_ref, out_ref, sems = refs
    far = unpack(far_ref[...])
    schur = cap_ref[...] - coupling * coupling * far
    t = refine_schur(schur, inv_ref[...])
    g_left = left_ref[...] + coupling * dot3(far, left_far_ref[...])
    g_right = right_ref[...] + coupling * dot3(far, right_far_ref[...])
    half = left_ref.shape[1]
    k_ref[:, :half] = dot3(t, g_left)
    k_ref[:, half:] = dot3(t, g_right)

    @pl.when(wide_ref[0, 0] > 0.5)
    def _():
        for g, columns in ((g_left, slice(None, half)), (g_right, slice(half, None))):
            k = k_ref[:, columns]
            k_ref[:, columns] = k + dot3(t, g - dot6(schur, k))

    k_high, k_low = halves(k_ref[...])
    pieces = sems.shape[0]
    rows = out_ref.shape[0] // pieces
    stores = []
    for i in range(pieces):
        block = slice(i * rows, (i + 1) * rows)
        high = high_ref[block]
        change = pass_dot(high, k_low, NN) + pass_dot(low_ref[block], k_high, NN)
        out_ref[block] = z1_ref[block] - pass_dot(high, k_high, NN) - change
        store = pltpu.make_async_copy(out_ref.at[block], out_hbm.at[block], sems.at[i])
        store.start()
        stores.append(store)
    for store in stores:
        store.wait()


def call(kernel, outs, *args, micros, scratch=(), space=pltpu.VMEM, out_space=pltpu.VMEM, grant=VMEM_BYTES):
    return pl.pallas_call(
        kernel,
        out_shape=[o if isinstance(o, jax.ShapeDtypeStruct) else jax.ShapeDtypeStruct(o, F32) for o in outs],
        in_specs=[pl.BlockSpec(memory_space=space)] * len(args),
        out_specs=[pl.BlockSpec(memory_space=out_space)] * len(outs),
        scratch_shapes=[pltpu.VMEM(x, F32) if isinstance(x, tuple) else x for x in scratch],
        compiler_params=pltpu.CompilerParams(vmem_limit_bytes=grant),
        cost_estimate=pl.CostEstimate(flops=int(micros * 1e9), bytes_accessed=int(micros * 3e6), transcendentals=0),
    )(*args)


def shards(level1_basis, level2_basis, probes):
    points, rank = level1_basis.shape
    part, columns = level2_basis.shape[0], probes.shape[1]
    coupling = points / 3.0
    n_cols = lax.axis_size("cols")
    square, tall, tile = (rank, rank), (rank, columns), (8, 128)
    packed = (3 * rank // 2, rank // 2)

    def run(kernel, outs, *args, **kw):
        return call(lambda *refs: kernel(coupling, *refs), outs, *args, **kw)

    def swap(value, bits, axis="rows"):
        return lax.ppermute(value, axis, [(i, i ^ bits) for i in range(lax.axis_size(axis))])

    def core_gather(value):
        groups = [[2 * i, 2 * i + 1] for i in range(n_cols // 2)]
        return lax.all_gather(value, "cols", axis=0, tiled=True, axis_index_groups=groups)

    cap, y, own_part = run(
        leaf_kernel,
        [square, tall, (part, points)],
        *(level1_basis, probes, level2_basis),
        micros=3,
        scratch=[(points, rank), (points, columns), pltpu.SemaphoreType.DMA((3,))],
        space=pltpu.HBM,
        grant=62 * 2**20,
    )
    far_part = swap(own_part, 2, "cols")
    other_y = swap(y, 1)
    inv, wide = run(invert_kernel, [square, tile], cap, micros=4, scratch=[(2 * rank, rank)])
    y2t = core_gather(jnp.concatenate([own_part, far_part], axis=0))
    bt, ht, sent = run(cross_kernel, [square] * 3, wide, level1_basis, y2t, cap, inv, micros=4)
    other_half = swap(sent, 1)
    side = (rank, columns // 2)
    dd, w, v_left, v_right = run(project_kernel, [square, tall, side, side], y2t, probes, y, ht, micros=3)
    other_v_left = swap(v_left, 1)
    other_v_right = swap(v_right, 1)
    other = core_gather(other_half)
    schur, t, et, p = run(pair_kernel, [square] * 3 + [packed], wide, cap, inv, bt, other, dd, micros=20)
    other_p = swap(p, 1)
    half = columns // 2

    def rhs(first, other_v):
        kernel = functools.partial(rhs_kernel, coupling, first)
        return call(kernel, [(rank, half)] * 2, wide, schur, t, et, y, other, other_y, w, other_v, micros=3)

    f_left, ez_left = rhs(0, other_v_left)
    far_left = swap(f_left, 3)
    f_right, ez_right = rhs(half, other_v_right)
    far_right = swap(f_right, 3)
    cap_two, inv_two, wide_two, sent_two = run(
        quad_kernel, [square, square, tile, packed], p, other_p, micros=6, scratch=[(2 * rank, rank)]
    )
    far_two = swap(sent_two, 3)
    bits = jax.ShapeDtypeStruct((points, rank), BF16)
    z1, high, low, updated = run(
        apply_kernel,
        [(points, columns), bits, bits, (part, points)],
        *(level1_basis, y2t, probes, et, ez_left, ez_right),
        micros=4,
        scratch=[(rank, points)],
    )
    (out,) = run(
        last_kernel,
        [(points, columns)],
        *(wide_two, cap_two, inv_two, far_two, f_left, f_right, far_left, far_right, z1, high, low),
        micros=7,
        scratch=[(rank, columns), (points, columns), pltpu.SemaphoreType.DMA((3,))],
        out_space=pltpu.HBM,
    )
    return out, updated


def solution(mesh):
    return jax.shard_map(
        shards,
        mesh=mesh,
        in_specs=(P("rows", None), P("cols", "rows"), P("rows", "cols")),
        out_specs=(P("rows", "cols"), P("cols", "rows")),
        check_vma=False,
    )
```
